32 devices in a mesh: branch: 2 (over x), head: 4 (over z), page: 4 (over y, core).
Axes of the slice: x: 2, y: 2, z: 4, core: 2. Of those that a mesh axis runs over, the one named last changes fastest.
Arguments:
- queries: bfloat16 [2048, 4096], P(('branch', 'page'), 'head'), may hold values from -6 to 6
- new_keys: bfloat16 [2048, 512], P(('branch', 'page'), 'head'), may hold values from -6 to 6
- new_values: bfloat16 [2048, 512], P(('branch', 'page'), 'head'), may hold values from -6 to 6
- cache_keys: bfloat16 [16, 64, 512], P(('branch', 'page'), None, 'head'), may hold values from -6 to 6
- cache_values: bfloat16 [16, 64, 512], P(('branch', 'page'), None, 'head'), may hold values from -6 to 6
- block_table: int32 [8, 4], P(('branch', 'page')), may hold values from 0 to 15, as said below
- ancestor_len: int32 [8], P(('branch', 'page')), may hold values from 64 to 256, as said below
- out_weight: bfloat16 [4096, 8192], P('head', 'page'), may hold values from -0.375 to 0.375
Outputs:
- layer_out: bfloat16 [2048, 8192], P(('branch', 'head'), 'page')
The draws below stay inside these ranges and needn't reach their ends.
Inputs may be any that keep to these rules, and one draw needn't show every extreme that they name: `block_table`: each row names 4 distinct page ids; its first 1 entries are the same for every branch. `ancestor_len`: every branch's ancestors fill its first 1 pages; some branch reaches the maximum.
All inputs are finite; a program needn't handle non-finite values.
Results may differ from the reference program's by a relative error of at most 0.018.
Values may be sent and summed in bfloat16 or wider, within the bound.
A program may use at most 64 MiB of HBM per device.

```python
import math
import jax
import jax.numpy as jnp
from jax import lax

D = 8192
H = 32
KVH = 4
HD = 128
PAGE_TOK = 64
NEW = 256
BRANCHES = 8
TOKENS = 2048
PAGES = 16
MAXP = 4
ROOT = 1
N_HEAD = 4


def draw_queries(key, part):
    values = jnp.clip(jax.random.normal(jax.random.fold_in(key, 7), (TOKENS, H * HD), jnp.float32), -6.0, 6.0)
    return values.astype(jnp.bfloat16)


def draw_new_keys(key, part):
    values = jnp.clip(jax.random.normal(jax.random.fold_in(key, 8), (TOKENS, KVH * HD), jnp.float32), -6.0, 6.0)
    return values.astype(jnp.bfloat16)


def draw_block_table(key, part):
    order = jax.random.permutation(jax.random.fold_in(key, 11), PAGES)
    shared = order[:ROOT]
    others = order[ROOT:]
    row_keys = jax.random.split(jax.random.fold_in(key, 12), BRANCHES)
    picks = jax.vmap(lambda row_key: jax.random.permutation(row_key, PAGES - ROOT))(row_keys)[:, :MAXP - ROOT]
    table = jnp.concatenate([jnp.broadcast_to(shared[None, :], (BRANCHES, ROOT)), others[picks]], 1)
    return table.astype(jnp.int32)


def draw_ancestor_len(key, part):
    lower = ROOT * PAGE_TOK
    extent = (MAXP - ROOT) * PAGE_TOK
    first_draw = jax.random.randint(jax.random.fold_in(key, 21), (BRANCHES,), 0, extent + 1)
    second_draw = jax.random.randint(jax.random.fold_in(key, 22), (BRANCHES,), 0, extent + 1)
    lengths = lower + first_draw * second_draw // extent
    deepest = jax.random.randint(jax.random.fold_in(key, 23), (), 0, BRANCHES)
    lengths = jnp.where(jnp.arange(BRANCHES) == deepest, MAXP * PAGE_TOK, lengths)
    return lengths.astype(jnp.int32)


def steps_of(stream_key, dims, cuts, least, high):
    factor_of, own = 1.0, jax.random.fold_in(stream_key, 6)
    for axis_at, parts in cuts:
        draws = jnp.exp(jax.random.uniform(jax.random.fold_in(own, axis_at), (parts,), jnp.float32, least / len(cuts), high / len(cuts)))
        factor_of = factor_of * jnp.repeat(draws, dims[axis_at] // parts).reshape([-1 if axis == axis_at else 1 for axis in range(len(dims))])
    return factor_of


def bell_draw(rng, shape, width, limit, shards=(), kind=jnp.bfloat16):
    loudness = steps_of(rng, shape, shards, -0.22, 0.18) if shards else 1.0
    array = jax.random.normal(rng, shape, jnp.float32) * width * loudness
    return jnp.minimum(jnp.maximum(array, -limit), limit).astype(kind)


def setup_inputs(seed: int = 0) -> dict:
    keys = jax.random.split(jax.random.key(seed), 9)
    return {
        "queries": draw_queries(jax.random.fold_in(keys[8], 71), 0),
        "new_keys": draw_new_keys(jax.random.fold_in(keys[8], 71), 0),
        "new_values": bell_draw(keys[2], (TOKENS, KVH * HD), 1.0, 6.0, ((0, 8), (1, 4))),
        "cache_keys": bell_draw(keys[3], (PAGES, PAGE_TOK, KVH * HD), 1.0, 6.0, ((0, 8), (2, 4))),
        "cache_values": bell_draw(keys[4], (PAGES, PAGE_TOK, KVH * HD), 1.0, 6.0, ((0, 8), (2, 4))),
        "block_table": draw_block_table(jax.random.fold_in(keys[8], 71), 0),
        "ancestor_len": draw_ancestor_len(jax.random.fold_in(keys[8], 71), 0),
        "out_weight": bell_draw(keys[7], (H * HD, D), (H * HD // 16) ** -0.5, 0.375, ((0, 4), (1, 4))),
    }


def reference(queries, new_keys, new_values, cache_keys, cache_values, block_table, ancestor_len, out_weight):
    group_size = H // KVH
    score_scale = 1.0 / math.sqrt(HD)
    query_blocks = queries.reshape(BRANCHES, NEW, KVH, group_size, HD)
    key_blocks = new_keys.reshape(BRANCHES, NEW, KVH, HD)
    value_blocks = new_values.reshape(BRANCHES, NEW, KVH, HD)
    cached_k = cache_keys.reshape(PAGES, PAGE_TOK, KVH, HD)
    cached_v = cache_values.reshape(PAGES, PAGE_TOK, KVH, HD)

    def per_branch(branch_data):
        branch_q, branch_k, branch_v, table_row, context = branch_data
        ancestor_k = cached_k[table_row].reshape(MAXP * PAGE_TOK, KVH, HD)
        ancestor_v = cached_v[table_row].reshape(MAXP * PAGE_TOK, KVH, HD)
        all_keys = jnp.concatenate([ancestor_k, branch_k], 0).astype(jnp.float32)
        all_values = jnp.concatenate([ancestor_v, branch_v], 0).astype(jnp.float32)
        positions = jnp.arange(MAXP * PAGE_TOK, dtype=jnp.int32)
        places = jnp.arange(NEW, dtype=jnp.int32)
        ancestor_mask = jnp.broadcast_to((positions < context)[None, :], (NEW, MAXP * PAGE_TOK))
        causal_mask = places[None, :] <= places[:, None]
        key_mask = jnp.concatenate([ancestor_mask, causal_mask], 1)
        scores = jnp.einsum('nkgd,lkd->kgnl', branch_q.astype(jnp.float32), all_keys) * score_scale
        masked = jnp.where(key_mask[None, None], scores, -1e+30)
        row_max = lax.optimization_barrier(jnp.max(masked, axis=-1, keepdims=True))
        numer = jnp.where(key_mask[None, None], jnp.exp(scores - row_max), 0.0).astype(jnp.bfloat16)
        denom = lax.optimization_barrier(jnp.sum(numer.astype(jnp.float32), axis=-1))
        summed = jnp.einsum('kgnl,lkd->nkgd', numer.astype(jnp.float32), all_values)
        attn = summed / jnp.transpose(denom, (2, 0, 1))[..., None]
        return attn.astype(jnp.bfloat16).reshape(NEW, H * HD)
    attn_all = lax.map(per_branch, (query_blocks, key_blocks, value_blocks, block_table, ancestor_len))
    attn_all = attn_all.reshape(TOKENS, H * HD)
    slice_width = H * HD // N_HEAD
    result = jnp.zeros((TOKENS, D), jnp.float32)
    for group_index in range(N_HEAD):
        lower = group_index * slice_width
        partial_term = jnp.dot(attn_all[:, lower:lower + slice_width], out_weight[lower:lower + slice_width], preferred_element_type=jnp.float32)
        result = result + partial_term.astype(jnp.bfloat16).astype(jnp.float32)
    return result.astype(jnp.bfloat16)
```

```python
import functools
import math

import jax
import jax.numpy as jnp
from jax import lax
from jax.experimental import pallas as pl
from jax.experimental.pallas import tpu as pltpu
from jax.sharding import PartitionSpec as P

HD = 128
PAGE_TOK = 64
NEW = 256
PAIR = 2
MESH = pl.DeviceIdType.MESH


def kernel(
    n_branch,
    n_head,
    n_page,
    width,
    table_ref,
    len_ref,
    q_ref,
    nk_ref,
    nv_ref,
    ck_ref,
    cv_ref,
    w_hbm,
    out_ref,
    k_all,
    v_all,
    k_cat,
    v_cat,
    attn_all,
    w_ref,
    flow,
    total,
    w_sem,
    kv_send,
    kv_recv,
    attn_send,
    attn_recv,
    flow_send,
    flow_recv,
):
    my_branch = lax.axis_index("branch")
    z = lax.axis_index("head")
    my_page = lax.axis_index("page")
    group = n_branch * n_page
    me = my_branch * n_page + my_page
    rows = q_ref.shape[0]
    heads = q_ref.shape[1] // HD
    branches, slots = table_ref.shape
    pages_here = ck_ref.shape[0]
    ancestors = slots * PAGE_TOK
    span = ancestors + NEW
    rows_out, columns = out_ref.shape
    chunks = columns // width
    pairs = heads // PAIR

    w_copy = pltpu.make_async_copy(w_hbm, w_ref, w_sem)
    w_copy.start()

    def peer_of(k):
        other = lax.rem(me + k, group)
        return other // n_page, lax.rem(other, n_page)

    barrier = pltpu.get_barrier_semaphore()

    @pl.loop(1, group)
    def _(k):
        b, p = peer_of(k)
        pl.semaphore_signal(
            barrier, inc=1, device_id={"branch": b, "page": p}, device_id_type=MESH
        )

    @pl.when(z > 0)
    def _():
        pl.semaphore_signal(barrier, inc=1, device_id={"head": z - 1}, device_id_type=MESH)

    @pl.when(z < n_head - 1)
    def _():
        pl.semaphore_signal(barrier, inc=1, device_id={"head": z + 1}, device_id_type=MESH)

    inner_head = jnp.logical_and(z > 0, z < n_head - 1)
    pl.semaphore_wait(barrier, group - 1 + jnp.where(inner_head, 2, 1))

    def cache_copy(which, k):
        b, p = peer_of(k)
        src, dst = ((ck_ref, k_all), (cv_ref, v_all))[which]
        return pltpu.make_async_remote_copy(
            src_ref=src,
            dst_ref=dst.at[pl.ds(me * pages_here, pages_here)],
            send_sem=kv_send.at[which, k],
            recv_sem=kv_recv.at[which, k],
            device_id={"branch": b, "page": p},
            device_id_type=MESH,
        )

    @pl.loop(1, group)
    def _(k):
        cache_copy(0, k).start()
        cache_copy(1, k).start()

    k_all[pl.ds(me * pages_here, pages_here)] = ck_ref[...]
    v_all[pl.ds(me * pages_here, pages_here)] = cv_ref[...]
    v_cat[:, HD:] = jnp.ones((span, HD), jnp.bfloat16)

    def attn_copy(j, k):
        p = lax.rem(my_page + k, n_page)
        piece = attn_all.at[
            pl.ds(pl.multiple_of(my_page * rows, rows), rows),
            pl.ds(pl.multiple_of(j * PAIR * HD, PAIR * HD), PAIR * HD),
        ]
        return pltpu.make_async_remote_copy(
            src_ref=piece,
            dst_ref=piece,
            send_sem=attn_send.at[k, j],
            recv_sem=attn_recv.at[k, j],
            device_id={"page": p},
            device_id_type=MESH,
        )

    @pl.loop(1, group)
    def _(k):
        cache_copy(0, k).wait_recv()
        cache_copy(1, k).wait_recv()

    scale = math.log2(math.e) / math.sqrt(HD)
    column = lax.broadcasted_iota(jnp.int32, (NEW, span), 1)
    row = lax.broadcasted_iota(jnp.int32, (NEW, span), 0)

    for b in range(branches):
        for s in range(slots):
            page_id = table_ref[b, s]
            k_cat[s * PAGE_TOK : (s + 1) * PAGE_TOK] = k_all[page_id]
            v_cat[s * PAGE_TOK : (s + 1) * PAGE_TOK, :HD] = v_all[page_id]
        k_cat[ancestors:] = nk_ref[b * NEW : (b + 1) * NEW]
        v_cat[ancestors:, :HD] = nv_ref[b * NEW : (b + 1) * NEW]
        bound = jnp.where(column < ancestors, len_ref[b], ancestors + 1 + row)
        bias = jnp.where(column < bound, 0.0, -1e30).astype(jnp.float32)

        @pl.loop(0, pairs)
        def _(j):
            for h in range(PAIR):
                lanes = pl.ds(pl.multiple_of((j * PAIR + h) * HD, HD), HD)
                scores = lax.dot_general(
                    q_ref[b * NEW : (b + 1) * NEW, lanes],
                    k_cat[...],
                    (((1,), (1,)), ((), ())),
                    preferred_element_type=jnp.float32,
                )
                scores = scores * scale + bias
                top = jnp.max(scores, axis=-1, keepdims=True)
                numer = jnp.exp2(scores - top).astype(jnp.bfloat16)
                mixed = jnp.dot(numer, v_cat[...], preferred_element_type=jnp.float32)
                place = pl.ds(pl.multiple_of(my_page * rows + b * NEW, NEW), NEW)
                attn_all[place, lanes] = (mixed[:, :HD] / mixed[:, HD:]).astype(jnp.bfloat16)
            if b == branches - 1:

                @pl.loop(1, n_page)
                def _(k):
                    attn_copy(j, k).start()

    w_copy.wait()

    def flow_copy(d, c):
        down = jnp.where(d < z, 1, 0)
        return pltpu.make_async_remote_copy(
            src_ref=flow.at[down, d, c],
            dst_ref=flow.at[down, d, c],
            send_sem=flow_send.at[d, c],
            recv_sem=flow_recv.at[down, d, c],
            device_id={"head": jnp.where(d < z, z - 1, z + 1)},
            device_id_type=MESH,
        )

    def incoming(down, d, c):
        return pltpu.make_async_remote_copy(
            src_ref=flow.at[down, d, c],
            dst_ref=flow.at[down, d, c],
            send_sem=flow_send.at[d, c],
            recv_sem=flow_recv.at[down, d, c],
            device_id={"head": jnp.where(z == 0, z + 1, z - 1)},
            device_id_type=MESH,
        )

    phases = n_head // 2
    pages_phase = n_page // phases
    my_phase = my_page // pages_phase

    for ph in range(phases):
        half = lax.rem(my_phase + ph, phases)

        @pl.loop(0, pages_phase)
        def _(i):
            source = half * pages_phase + i
            k = lax.rem(my_page - source + n_page, n_page)

            @pl.when(k > 0)
            def _():
                @pl.loop(0, pairs)
                def _(j):
                    piece = attn_all.at[
                        pl.ds(pl.multiple_of(source * rows, rows), rows),
                        pl.ds(pl.multiple_of(j * PAIR * HD, PAIR * HD), PAIR * HD),
                    ]
                    pltpu.make_async_remote_copy(
                        src_ref=piece,
                        dst_ref=piece,
                        send_sem=attn_send.at[k, j],
                        recv_sem=attn_recv.at[k, j],
                        device_id={"page": lax.rem(my_page + 1, n_page)},
                        device_id_type=MESH,
                    ).wait_recv()

        @pl.loop(0, chunks * 2)
        def _(step):
            c = step // 2
            i = lax.rem(step, 2)
            d = half * 2 + jnp.where(z < n_head // 2, 1 - i, i)
            part = jnp.dot(
                attn_all[pl.ds(pl.multiple_of(d * rows_out, rows_out), rows_out), :],
                w_ref[:, pl.ds(pl.multiple_of(c * width, width), width)],
                preferred_element_type=jnp.float32,
            )
            down = jnp.where(d < z, 1, 0)
            received = jnp.where(d < z, z < n_head - 1, z > 0)

            @pl.when(d == z)
            def _():
                total[c] = part

            @pl.when(jnp.logical_and(d != z, received))
            def _():
                incoming(down, d, c).wait_recv()
                flow[down, d, c] = (part + flow[down, d, c].astype(jnp.float32)).astype(
                    jnp.bfloat16
                )
                flow_copy(d, c).start()

            @pl.when(jnp.logical_and(d != z, jnp.logical_not(received)))
            def _():
                flow[down, d, c] = part.astype(jnp.bfloat16)
                flow_copy(d, c).start()

    @pl.loop(0, chunks)
    def _(c):
        @pl.when(z > 0)
        def _():
            incoming(0, z, c).wait_recv()
            total[c] = total[c] + flow[0, z, c].astype(jnp.float32)

        @pl.when(z < n_head - 1)
        def _():
            incoming(1, z, c).wait_recv()
            total[c] = total[c] + flow[1, z, c].astype(jnp.float32)

        out_ref[:, pl.ds(pl.multiple_of(c * width, width), width)] = total[c].astype(
            jnp.bfloat16
        )

    @pl.loop(1, group)
    def _(k):
        cache_copy(0, k).wait_send()
        cache_copy(1, k).wait_send()

    @pl.loop(1, n_page)
    def _(k):
        @pl.loop(0, pairs)
        def _(j):
            attn_copy(j, k).wait_send()

    @pl.loop(0, n_head * chunks)
    def _(step):
        d = step // chunks
        c = lax.rem(step, chunks)

        @pl.when(d != z)
        def _():
            flow_copy(d, c).wait_send()


def solution(mesh):
    n_branch, n_head, n_page = (mesh.shape[a] for a in ("branch", "head", "page"))

    def shards(
        queries,
        new_keys,
        new_values,
        cache_keys,
        cache_values,
        block_table,
        ancestor_len,
        out_weight,
    ):
        rows, inner = queries.shape
        columns = out_weight.shape[1]
        rows_out = rows * n_page // n_head
        pages = cache_keys.shape[0] * n_branch * n_page
        span = block_table.shape[1] * PAGE_TOK + NEW
        width = math.gcd(columns, 256)
        chunks = columns // width
        pairs = inner // HD // PAIR
        group = n_branch * n_page
        vmem = pl.BlockSpec(memory_space=pltpu.VMEM)
        smem = pl.BlockSpec(memory_space=pltpu.SMEM)
        hbm = pl.BlockSpec(memory_space=pl.ANY)
        return pl.pallas_call(
            functools.partial(kernel, n_branch, n_head, n_page, width),
            out_shape=jax.ShapeDtypeStruct((rows_out, columns), jnp.bfloat16),
            in_specs=[smem, smem, vmem, vmem, vmem, vmem, vmem, hbm],
            out_specs=vmem,
            scratch_shapes=[
                pltpu.VMEM((pages, PAGE_TOK, HD), jnp.bfloat16),
                pltpu.VMEM((pages, PAGE_TOK, HD), jnp.bfloat16),
                pltpu.VMEM((span, HD), jnp.bfloat16),
                pltpu.VMEM((span, 2 * HD), jnp.bfloat16),
                pltpu.VMEM((rows * n_page, inner), jnp.bfloat16),
                pltpu.VMEM(out_weight.shape, jnp.bfloat16),
                pltpu.VMEM((2, n_head, chunks, rows_out, width), jnp.bfloat16),
                pltpu.VMEM((chunks, rows_out, width), jnp.float32),
                pltpu.SemaphoreType.DMA,
                pltpu.SemaphoreType.DMA((2, group)),
                pltpu.SemaphoreType.DMA((2, group)),
                pltpu.SemaphoreType.DMA((n_page, pairs)),
                pltpu.SemaphoreType.DMA((n_page, pairs)),
                pltpu.SemaphoreType.DMA((n_head, chunks)),
                pltpu.SemaphoreType.DMA((2, n_head, chunks)),
            ],
            compiler_params=pltpu.CompilerParams(
                collective_id=0, has_side_effects=True, vmem_limit_bytes=60 * 1024 * 1024
            ),
            cost_estimate=pl.CostEstimate(
                flops=2 * rows * n_page * inner * columns,
                bytes_accessed=2 * (inner * columns + rows_out * columns),
                transcendentals=0,
            ),
        )(
            block_table,
            ancestor_len,
            queries,
            new_keys,
            new_values,
            cache_keys,
            cache_values,
            out_weight,
        )

    in_specs = (
        P(("branch", "page"), "head"),
        P(("branch", "page"), "head"),
        P(("branch", "page"), "head"),
        P(("branch", "page"), None, "head"),
        P(("branch", "page"), None, "head"),
        P(("branch", "page"), None),
        P(("branch", "page")),
        P("head", "page"),
    )
    out_specs = P(("branch", "head"), "page")
    return jax.shard_map(shards, mesh=mesh, in_specs=in_specs, out_specs=out_specs, check_vma=False)
```

```python
import functools
import math

import jax
import jax.numpy as jnp
from jax import lax
from jax.experimental import pallas as pl
from jax.experimental.pallas import tpu as pltpu
from jax.sharding import PartitionSpec as P

HD = 128
PAGE_TOK = 64
NEW = 256
PAIR = 2
MESH = pl.DeviceIdType.MESH


def kernel(
    n_branch,
    n_head,
    n_page,
    width,
    table_ref,
    len_ref,
    q_ref,
    nk_ref,
    nv_ref,
    ck_ref,
    cv_ref,
    w_hbm,
    out_ref,
    k_all,
    v_all,
    k_cat,
    v_cat,
    attn_all,
    w_ref,
    flow,
    total,
    w_sem,
    kv_send,
    kv_recv,
    attn_send,
    attn_recv,
    flow_send,
    flow_recv,
):
    my_branch = lax.axis_index("branch")
    z = lax.axis_index("head")
    my_page = lax.axis_index("page")
    group = n_branch * n_page
    me = my_branch * n_page + my_page
    rows = q_ref.shape[0]
    heads = q_ref.shape[1] // HD
    branches, slots = table_ref.shape
    pages_here = ck_ref.shape[0]
    ancestors = slots * PAGE_TOK
    span = ancestors + NEW
    rows_out, columns = out_ref.shape
    chunks = columns // width
    pairs = heads // PAIR

    w_copy = pltpu.make_async_copy(w_hbm, w_ref, w_sem)
    w_copy.start()

    def peer_of(k):
        other = lax.rem(me + k, group)
        return other // n_page, lax.rem(other, n_page)

    barrier = pltpu.get_barrier_semaphore()

    @pl.loop(1, group)
    def _(k):
        b, p = peer_of(k)
        pl.semaphore_signal(
            barrier, inc=1, device_id={"branch": b, "page": p}, device_id_type=MESH
        )

    @pl.when(z > 0)
    def _():
        pl.semaphore_signal(barrier, inc=1, device_id={"head": z - 1}, device_id_type=MESH)

    @pl.when(z < n_head - 1)
    def _():
        pl.semaphore_signal(barrier, inc=1, device_id={"head": z + 1}, device_id_type=MESH)

    inner_head = jnp.logical_and(z > 0, z < n_head - 1)
    pl.semaphore_wait(barrier, group - 1 + jnp.where(inner_head, 2, 1))

    def cache_copy(which, k):
        b, p = peer_of(k)
        src, dst = ((ck_ref, k_all), (cv_ref, v_all))[which]
        return pltpu.make_async_remote_copy(
            src_ref=src,
            dst_ref=dst.at[pl.ds(me * pages_here, pages_here)],
            send_sem=kv_send.at[which, k],
            recv_sem=kv_recv.at[which, k],
            device_id={"branch": b, "page": p},
            device_id_type=MESH,
        )

    @pl.loop(1, group)
    def _(k):
        cache_copy(0, k).start()
        cache_copy(1, k).start()

    k_all[pl.ds(me * pages_here, pages_here)] = ck_ref[...]
    v_all[pl.ds(me * pages_here, pages_here)] = cv_ref[...]
    v_cat[:, HD:] = jnp.ones((span, HD), jnp.bfloat16)

    def attn_copy(j, k):
        p = lax.rem(my_page + k, n_page)
        piece = attn_all.at[
            pl.ds(pl.multiple_of(my_page * rows, rows), rows),
            pl.ds(pl.multiple_of(j * PAIR * HD, PAIR * HD), PAIR * HD),
        ]
        return pltpu.make_async_remote_copy(
            src_ref=piece,
            dst_ref=piece,
            send_sem=attn_send.at[k, j],
            recv_sem=attn_recv.at[k, j],
            device_id={"page": p},
            device_id_type=MESH,
        )

    @pl.loop(1, group)
    def _(k):
        cache_copy(0, k).wait_recv()
        cache_copy(1, k).wait_recv()

    scale = math.log2(math.e) / math.sqrt(HD)
    column = lax.broadcasted_iota(jnp.int32, (NEW, span), 1)
    row = lax.broadcasted_iota(jnp.int32, (NEW, span), 0)

    for b in range(branches):
        for s in range(slots):
            page_id = table_ref[b, s]
            k_cat[s * PAGE_TOK : (s + 1) * PAGE_TOK] = k_all[page_id]
            v_cat[s * PAGE_TOK : (s + 1) * PAGE_TOK, :HD] = v_all[page_id]
        k_cat[ancestors:] = nk_ref[b * NEW : (b + 1) * NEW]
        v_cat[ancestors:, :HD] = nv_ref[b * NEW : (b + 1) * NEW]
        bound = jnp.where(column < ancestors, len_ref[b], ancestors + 1 + row)
        bias = jnp.where(column < bound, 0.0, -1e30).astype(jnp.float32)

        @pl.loop(0, pairs)
        def _(j):
            for h in range(PAIR):
                lanes = pl.ds(pl.multiple_of((j * PAIR + h) * HD, HD), HD)
                scores = lax.dot_general(
                    q_ref[b * NEW : (b + 1) * NEW, lanes],
                    k_cat[...],
                    (((1,), (1,)), ((), ())),
                    preferred_element_type=jnp.float32,
                )
                scores = scores * scale + bias
                top = jnp.max(scores, axis=-1, keepdims=True)
                numer = jnp.exp2(scores - top).astype(jnp.bfloat16)
                mixed = jnp.dot(numer, v_cat[...], preferred_element_type=jnp.float32)
                place = pl.ds(pl.multiple_of(my_page * rows + b * NEW, NEW), NEW)
                attn_all[place, lanes] = (mixed[:, :HD] / mixed[:, HD:]).astype(jnp.bfloat16)
            if b == branches - 1:

                @pl.loop(1, n_page)
                def _(k):
                    attn_copy(j, k).start()

    w_copy.wait()

    def flow_copy(d, c):
        down = jnp.where(d < z, 1, 0)
        return pltpu.make_async_remote_copy(
            src_ref=flow.at[down, d, c],
            dst_ref=flow.at[down, d, c],
            send_sem=flow_send.at[d, c],
            recv_sem=flow_recv.at[down, d, c],
            device_id={"head": jnp.where(d < z, z - 1, z + 1)},
            device_id_type=MESH,
        )

    def incoming(down, d, c):
        return pltpu.make_async_remote_copy(
            src_ref=flow.at[down, d, c],
            dst_ref=flow.at[down, d, c],
            send_sem=flow_send.at[d, c],
            recv_sem=flow_recv.at[down, d, c],
            device_id={"head": jnp.where(z == 0, z + 1, z - 1)},
            device_id_type=MESH,
        )

    phases = n_head // 2
    pages_phase = n_page // phases
    my_phase = my_page // pages_phase
    ticks = (n_head - 1) * chunks

    def stream(tick, going_down):
        dest = piece = jnp.int32(0)
        for first in range(phases):
            start = 0
            for ph in range(phases):
                half = (first + ph) % phases
                dests = [half * 2, half * 2 + 1] if going_down else [half * 2 + 1, half * 2]
                dests = [d for d in dests if d != (n_head - 1 if going_down else 0)]
                here = jnp.logical_and(my_phase == first, tick >= start)
                local = jnp.maximum(tick - start, 0)
                step = 1 if going_down else -1
                dest = jnp.where(here, dests[0] + step * lax.rem(local, len(dests)), dest)
                piece = jnp.where(here, local // len(dests), piece)
                start += len(dests) * chunks
        return dest, piece

    def wait_attention(first, count):
        @pl.loop(0, count)
        def _(i):
            source = lax.rem(first + i, n_page)
            k = lax.rem(my_page - source + n_page, n_page)

            @pl.when(k > 0)
            def _():
                @pl.loop(0, pairs)
                def _(j):
                    piece = attn_all.at[
                        pl.ds(pl.multiple_of(source * rows, rows), rows),
                        pl.ds(pl.multiple_of(j * PAIR * HD, PAIR * HD), PAIR * HD),
                    ]
                    pltpu.make_async_remote_copy(
                        src_ref=piece,
                        dst_ref=piece,
                        send_sem=attn_send.at[k, j],
                        recv_sem=attn_recv.at[k, j],
                        device_id={"page": lax.rem(my_page + 1, n_page)},
                        device_id_type=MESH,
                    ).wait_recv()

    def project(d, c):
        return jnp.dot(
            attn_all[pl.ds(pl.multiple_of(d * rows_out, rows_out), rows_out), :],
            w_ref[:, pl.ds(pl.multiple_of(c * width, width), width)],
            preferred_element_type=jnp.float32,
        )

    def event(tick, down):
        d, c = stream(tick, down)
        active = d < z if down == 1 else d > z
        received = z < n_head - 1 if down == 1 else z > 0
        mine = jnp.logical_and(d == z, z == 0) if down == 1 else d == z

        @pl.when(mine)
        def _():
            total[c] = project(d, c)

        @pl.when(jnp.logical_and(active, received))
        def _():
            part = project(d, c)
            incoming(down, d, c).wait_recv()
            flow[down, d, c] = (part + flow[down, d, c].astype(jnp.float32)).astype(
                jnp.bfloat16
            )
            flow_copy(d, c).start()

        @pl.when(jnp.logical_and(active, jnp.logical_not(received)))
        def _():
            flow[down, d, c] = project(d, c).astype(jnp.bfloat16)
            flow_copy(d, c).start()

    def run(low, high):
        @pl.loop(low, high)
        def _(tick):
            @pl.when(z < n_head // 2)
            def _():
                event(tick, 0)

            event(tick, 1)

            @pl.when(z >= n_head // 2)
            def _():
                event(tick, 0)

    wait_attention(my_phase * pages_phase, pages_phase)
    run(0, chunks)
    wait_attention((my_phase + 1) * pages_phase, n_page - pages_phase)
    run(chunks, ticks)

    @pl.loop(0, chunks)
    def _(c):
        @pl.when(z > 0)
        def _():
            incoming(0, z, c).wait_recv()
            total[c] = total[c] + flow[0, z, c].astype(jnp.float32)

        @pl.when(z < n_head - 1)
        def _():
            incoming(1, z, c).wait_recv()
            total[c] = total[c] + flow[1, z, c].astype(jnp.float32)

        out_ref[:, pl.ds(pl.multiple_of(c * width, width), width)] = total[c].astype(
            jnp.bfloat16
        )

    @pl.loop(1, group)
    def _(k):
        cache_copy(0, k).wait_send()
        cache_copy(1, k).wait_send()

    @pl.loop(1, n_page)
    def _(k):
        @pl.loop(0, pairs)
        def _(j):
            attn_copy(j, k).wait_send()

    @pl.loop(0, n_head * chunks)
    def _(step):
        d = step // chunks
        c = lax.rem(step, chunks)

        @pl.when(d != z)
        def _():
            flow_copy(d, c).wait_send()


def solution(mesh):
    n_branch, n_head, n_page = (mesh.shape[a] for a in ("branch", "head", "page"))

    def shards(
        queries,
        new_keys,
        new_values,
        cache_keys,
        cache_values,
        block_table,
        ancestor_len,
        out_weight,
    ):
        rows, inner = queries.shape
        columns = out_weight.shape[1]
        rows_out = rows * n_page // n_head
        pages = cache_keys.shape[0] * n_branch * n_page
        span = block_table.shape[1] * PAGE_TOK + NEW
        width = math.gcd(columns, 256)
        chunks = columns // width
        pairs = inner // HD // PAIR
        group = n_branch * n_page
        vmem = pl.BlockSpec(memory_space=pltpu.VMEM)
        smem = pl.BlockSpec(memory_space=pltpu.SMEM)
        hbm = pl.BlockSpec(memory_space=pl.ANY)
        return pl.pallas_call(
            functools.partial(kernel, n_branch, n_head, n_page, width),
            out_shape=jax.ShapeDtypeStruct((rows_out, columns), jnp.bfloat16),
            in_specs=[smem, smem, vmem, vmem, vmem, vmem, vmem, hbm],
            out_specs=vmem,
            scratch_shapes=[
                pltpu.VMEM((pages, PAGE_TOK, HD), jnp.bfloat16),
                pltpu.VMEM((pages, PAGE_TOK, HD), jnp.bfloat16),
                pltpu.VMEM((span, HD), jnp.bfloat16),
                pltpu.VMEM((span, 2 * HD), jnp.bfloat16),
                pltpu.VMEM((rows * n_page, inner), jnp.bfloat16),
                pltpu.VMEM(out_weight.shape, jnp.bfloat16),
                pltpu.VMEM((2, n_head, chunks, rows_out, width), jnp.bfloat16),
                pltpu.VMEM((chunks, rows_out, width), jnp.float32),
                pltpu.SemaphoreType.DMA,
                pltpu.SemaphoreType.DMA((2, group)),
                pltpu.SemaphoreType.DMA((2, group)),
                pltpu.SemaphoreType.DMA((n_page, pairs)),
                pltpu.SemaphoreType.DMA((n_page, pairs)),
                pltpu.SemaphoreType.DMA((n_head, chunks)),
                pltpu.SemaphoreType.DMA((2, n_head, chunks)),
            ],
            compiler_params=pltpu.CompilerParams(
                collective_id=0, has_side_effects=True, vmem_limit_bytes=60 * 1024 * 1024
            ),
            cost_estimate=pl.CostEstimate(
                flops=2 * rows * n_page * inner * columns,
                bytes_accessed=2 * (inner * columns + rows_out * columns),
                transcendentals=0,
            ),
        )(
            block_table,
            ancestor_len,
            queries,
            new_keys,
            new_values,
            cache_keys,
            cache_values,
            out_weight,
        )

    in_specs = (
        P(("branch", "page"), "head"),
        P(("branch", "page"), "head"),
        P(("branch", "page"), "head"),
        P(("branch", "page"), None, "head"),
        P(("branch", "page"), None, "head"),
        P(("branch", "page"), None),
        P(("branch", "page")),
        P("head", "page"),
    )
    out_specs = P(("branch", "head"), "page")
    return jax.shard_map(shards, mesh=mesh, in_specs=in_specs, out_specs=out_specs, check_vma=False)
```

```python
import functools
import math

import jax
import jax.numpy as jnp
from jax import lax
from jax.experimental import pallas as pl
from jax.experimental.pallas import tpu as pltpu
from jax.sharding import PartitionSpec as P

HD = 128
PAGE_TOK = 64
NEW = 256
PAIR = 2
SKEW = 2
MESH = pl.DeviceIdType.MESH


def kernel(
    n_branch,
    n_head,
    n_page,
    width,
    table_ref,
    len_ref,
    q_ref,
    nk_ref,
    nv_ref,
    ck_ref,
    cv_ref,
    w_hbm,
    out_ref,
    k_all,
    v_all,
    k_cat,
    v_cat,
    v_own,
    own_mix,
    own_top,
    attn_all,
    w_ref,
    flow,
    total,
    w_sem,
    kv_send,
    kv_recv,
    attn_send,
    attn_recv,
    flow_send,
    flow_recv,
):
    my_branch = lax.axis_index("branch")
    z = lax.axis_index("head")
    my_page = lax.axis_index("page")
    group = n_branch * n_page
    me = my_branch * n_page + my_page
    rows = q_ref.shape[0]
    heads = q_ref.shape[1] // HD
    branches, slots = table_ref.shape
    pages_here = ck_ref.shape[0]
    ancestors = slots * PAGE_TOK
    rows_out, columns = out_ref.shape
    chunks = columns // width
    pairs = heads // PAIR

    w_copy = pltpu.make_async_copy(w_hbm, w_ref, w_sem)
    w_copy.start()

    def peer_of(k):
        other = lax.rem(me + k, group)
        return other // n_page, lax.rem(other, n_page)

    barrier = pltpu.get_barrier_semaphore()

    @pl.loop(1, group)
    def _(k):
        b, p = peer_of(k)
        pl.semaphore_signal(
            barrier, inc=1, device_id={"branch": b, "page": p}, device_id_type=MESH
        )

    @pl.when(z > 0)
    def _():
        pl.semaphore_signal(barrier, inc=1, device_id={"head": z - 1}, device_id_type=MESH)

    @pl.when(z < n_head - 1)
    def _():
        pl.semaphore_signal(barrier, inc=1, device_id={"head": z + 1}, device_id_type=MESH)

    inner_head = jnp.logical_and(z > 0, z < n_head - 1)
    pl.semaphore_wait(barrier, group - 1 + jnp.where(inner_head, 2, 1))

    def cache_copy(which, k):
        b, p = peer_of(k)
        src, dst = ((ck_ref, k_all), (cv_ref, v_all))[which]
        return pltpu.make_async_remote_copy(
            src_ref=src,
            dst_ref=dst.at[pl.ds(me * pages_here, pages_here)],
            send_sem=kv_send.at[which, k],
            recv_sem=kv_recv.at[which, k],
            device_id={"branch": b, "page": p},
            device_id_type=MESH,
        )

    @pl.loop(1, group)
    def _(k):
        cache_copy(0, k).start()
        cache_copy(1, k).start()

    k_all[pl.ds(me * pages_here, pages_here)] = ck_ref[...]
    v_all[pl.ds(me * pages_here, pages_here)] = cv_ref[...]
    v_cat[:, HD:] = jnp.ones((ancestors, HD), jnp.bfloat16)

    scale = math.log2(math.e) / math.sqrt(HD)

    def softmax_part(scores, floor):
        top = jnp.max(scores, axis=-1, keepdims=True)
        if floor is not None:
            top = jnp.maximum(top, floor)
        return top, jnp.exp2(scores - top).astype(jnp.bfloat16)

    def scores_of(b, lanes, keys):
        return scale * lax.dot_general(
            q_ref[b * NEW : (b + 1) * NEW, lanes],
            keys,
            (((1,), (1,)), ((), ())),
            preferred_element_type=jnp.float32,
        )

    own_row = lax.broadcasted_iota(jnp.int32, (NEW, NEW), 0)
    own_column = lax.broadcasted_iota(jnp.int32, (NEW, NEW), 1)
    own_bias = jnp.where(own_column <= own_row, 0.0, -1e30).astype(jnp.float32)

    for b in range(branches):
        v_own[b, :, :HD] = nv_ref[b * NEW : (b + 1) * NEW]
        v_own[b, :, HD:] = jnp.ones((NEW, HD), jnp.bfloat16)

        @pl.loop(0, pairs)
        def _(j):
            for h in range(PAIR):
                head = j * PAIR + h
                lanes = pl.ds(pl.multiple_of(head * HD, HD), HD)
                top, numer = softmax_part(
                    scores_of(b, lanes, nk_ref[b * NEW : (b + 1) * NEW]) + own_bias, None
                )
                own_mix[b, head] = jnp.dot(numer, v_own[b], preferred_element_type=jnp.float32)
                own_top[b, head] = jnp.broadcast_to(top, (NEW, HD))

    def attn_copy(j, k):
        p = lax.rem(my_page + k, n_page)
        piece = attn_all.at[
            pl.ds(pl.multiple_of(my_page * rows, rows), rows),
            pl.ds(pl.multiple_of(j * PAIR * HD, PAIR * HD), PAIR * HD),
        ]
        return pltpu.make_async_remote_copy(
            src_ref=piece,
            dst_ref=piece,
            send_sem=attn_send.at[k, j],
            recv_sem=attn_recv.at[k, j],
            device_id={"page": p},
            device_id_type=MESH,
        )

    @pl.loop(1, group)
    def _(k):
        cache_copy(0, k).wait_recv()
        cache_copy(1, k).wait_recv()

    column = lax.broadcasted_iota(jnp.int32, (NEW, ancestors), 1)

    for b in range(branches):
        for s in range(slots):
            page_id = table_ref[b, s]
            k_cat[s * PAGE_TOK : (s + 1) * PAGE_TOK] = k_all[page_id]
            v_cat[s * PAGE_TOK : (s + 1) * PAGE_TOK, :HD] = v_all[page_id]
        bias = jnp.where(column < len_ref[b], 0.0, -1e30).astype(jnp.float32)

        @pl.loop(0, pairs)
        def _(j):
            for h in range(PAIR):
                head = j * PAIR + h
                lanes = pl.ds(pl.multiple_of(head * HD, HD), HD)
                before = own_top[b, head][:, :1]
                top, numer = softmax_part(scores_of(b, lanes, k_cat[...]) + bias, before)
                mixed = jnp.dot(numer, v_cat[...], preferred_element_type=jnp.float32)
                mixed = mixed + own_mix[b, head] * jnp.exp2(before - top)
                place = pl.ds(pl.multiple_of(my_page * rows + b * NEW, NEW), NEW)
                attn_all[place, lanes] = (mixed[:, :HD] / mixed[:, HD:]).astype(jnp.bfloat16)
            if b == branches - 1:

                @pl.loop(1, n_page)
                def _(k):
                    attn_copy(j, k).start()

    w_copy.wait()

    def flow_copy(d, c):
        down = jnp.where(d < z, 1, 0)
        return pltpu.make_async_remote_copy(
            src_ref=flow.at[down, d, c],
            dst_ref=flow.at[down, d, c],
            send_sem=flow_send.at[d, c],
            recv_sem=flow_recv.at[down, d, c],
            device_id={"head": jnp.where(d < z, z - 1, z + 1)},
            device_id_type=MESH,
        )

    def incoming(down, d, c):
        return pltpu.make_async_remote_copy(
            src_ref=flow.at[down, d, c],
            dst_ref=flow.at[down, d, c],
            send_sem=flow_send.at[d, c],
            recv_sem=flow_recv.at[down, d, c],
            device_id={"head": jnp.where(z == 0, z + 1, z - 1)},
            device_id_type=MESH,
        )

    phases = n_head // 2
    pages_phase = n_page // phases
    my_phase = my_page // pages_phase
    ticks = (n_head - 1) * chunks

    def stream(tick, going_down):
        dest = piece = jnp.int32(0)
        for first in range(phases):
            start = 0
            for ph in range(phases):
                half = (first + ph) % phases
                dests = [half * 2, half * 2 + 1] if going_down else [half * 2 + 1, half * 2]
                dests = [d for d in dests if d != (n_head - 1 if going_down else 0)]
                here = jnp.logical_and(my_phase == first, tick >= start)
                local = jnp.maximum(tick - start, 0)
                step = 1 if going_down else -1
                dest = jnp.where(here, dests[0] + step * lax.rem(local, len(dests)), dest)
                piece = jnp.where(here, local // len(dests), piece)
                start += len(dests) * chunks
        return dest, piece

    def wait_attention(first, count):
        @pl.loop(0, count)
        def _(i):
            source = lax.rem(first + i, n_page)
            k = lax.rem(my_page - source + n_page, n_page)

            @pl.when(k > 0)
            def _():
                @pl.loop(0, pairs)
                def _(j):
                    piece = attn_all.at[
                        pl.ds(pl.multiple_of(source * rows, rows), rows),
                        pl.ds(pl.multiple_of(j * PAIR * HD, PAIR * HD), PAIR * HD),
                    ]
                    pltpu.make_async_remote_copy(
                        src_ref=piece,
                        dst_ref=piece,
                        send_sem=attn_send.at[k, j],
                        recv_sem=attn_recv.at[k, j],
                        device_id={"page": lax.rem(my_page + 1, n_page)},
                        device_id_type=MESH,
                    ).wait_recv()

    def project(d, c):
        return jnp.dot(
            attn_all[pl.ds(pl.multiple_of(d * rows_out, rows_out), rows_out), :],
            w_ref[:, pl.ds(pl.multiple_of(c * width, width), width)],
            preferred_element_type=jnp.float32,
        )

    def event(step, down):
        depth = n_head - 1 - z if down == 1 else z
        tick = step - SKEW * jnp.maximum(depth - 1, 0)
        d, c = stream(tick, down)
        valid = jnp.logical_and(tick >= 0, tick < ticks)
        active = jnp.logical_and(valid, d < z if down == 1 else d > z)
        received = z < n_head - 1 if down == 1 else z > 0
        mine = jnp.logical_and(valid, d == z)
        if down == 1:
            mine = jnp.logical_and(mine, z == 0)

        @pl.when(mine)
        def _():
            total[c] = project(d, c)

        @pl.when(jnp.logical_and(active, received))
        def _():
            part = project(d, c)
            incoming(down, d, c).wait_recv()
            flow[down, d, c] = (part + flow[down, d, c].astype(jnp.float32)).astype(
                jnp.bfloat16
            )
            flow_copy(d, c).start()

        @pl.when(jnp.logical_and(active, jnp.logical_not(received)))
        def _():
            flow[down, d, c] = project(d, c).astype(jnp.bfloat16)
            flow_copy(d, c).start()

    def run(low, high):
        @pl.loop(low, high)
        def _(step):
            @pl.when(z < n_head // 2)
            def _():
                event(step, 0)

            event(step, 1)

            @pl.when(z >= n_head // 2)
            def _():
                event(step, 0)

    wait_attention(my_phase * pages_phase, pages_phase)
    run(0, chunks)
    wait_attention((my_phase + 1) * pages_phase, n_page - pages_phase)
    run(chunks, ticks + SKEW * (n_head - 2))

    @pl.loop(0, chunks)
    def _(c):
        @pl.when(z > 0)
        def _():
            incoming(0, z, c).wait_recv()
            total[c] = total[c] + flow[0, z, c].astype(jnp.float32)

        @pl.when(z < n_head - 1)
        def _():
            incoming(1, z, c).wait_recv()
            total[c] = total[c] + flow[1, z, c].astype(jnp.float32)

        out_ref[:, pl.ds(pl.multiple_of(c * width, width), width)] = total[c].astype(
            jnp.bfloat16
        )

    @pl.loop(1, group)
    def _(k):
        cache_copy(0, k).wait_send()
        cache_copy(1, k).wait_send()

    @pl.loop(1, n_page)
    def _(k):
        @pl.loop(0, pairs)
        def _(j):
            attn_copy(j, k).wait_send()

    @pl.loop(0, n_head * chunks)
    def _(step):
        d = step // chunks
        c = lax.rem(step, chunks)

        @pl.when(d != z)
        def _():
            flow_copy(d, c).wait_send()


def solution(mesh):
    n_branch, n_head, n_page = (mesh.shape[a] for a in ("branch", "head", "page"))

    def shards(
        queries,
        new_keys,
        new_values,
        cache_keys,
        cache_values,
        block_table,
        ancestor_len,
        out_weight,
    ):
        rows, inner = queries.shape
        columns = out_weight.shape[1]
        rows_out = rows * n_page // n_head
        pages = cache_keys.shape[0] * n_branch * n_page
        ancestors = block_table.shape[1] * PAGE_TOK
        branches = block_table.shape[0]
        heads = inner // HD
        width = math.gcd(columns, 256)
        chunks = columns // width
        pairs = inner // HD // PAIR
        group = n_branch * n_page
        vmem = pl.BlockSpec(memory_space=pltpu.VMEM)
        smem = pl.BlockSpec(memory_space=pltpu.SMEM)
        hbm = pl.BlockSpec(memory_space=pl.ANY)
        return pl.pallas_call(
            functools.partial(kernel, n_branch, n_head, n_page, width),
            out_shape=jax.ShapeDtypeStruct((rows_out, columns), jnp.bfloat16),
            in_specs=[smem, smem, vmem, vmem, vmem, vmem, vmem, hbm],
            out_specs=vmem,
            scratch_shapes=[
                pltpu.VMEM((pages, PAGE_TOK, HD), jnp.bfloat16),
                pltpu.VMEM((pages, PAGE_TOK, HD), jnp.bfloat16),
                pltpu.VMEM((ancestors, HD), jnp.bfloat16),
                pltpu.VMEM((ancestors, 2 * HD), jnp.bfloat16),
                pltpu.VMEM((branches, NEW, 2 * HD), jnp.bfloat16),
                pltpu.VMEM((branches, heads, NEW, 2 * HD), jnp.float32),
                pltpu.VMEM((branches, heads, NEW, HD), jnp.float32),
                pltpu.VMEM((rows * n_page, inner), jnp.bfloat16),
                pltpu.VMEM(out_weight.shape, jnp.bfloat16),
                pltpu.VMEM((2, n_head, chunks, rows_out, width), jnp.bfloat16),
                pltpu.VMEM((chunks, rows_out, width), jnp.float32),
                pltpu.SemaphoreType.DMA,
                pltpu.SemaphoreType.DMA((2, group)),
                pltpu.SemaphoreType.DMA((2, group)),
                pltpu.SemaphoreType.DMA((n_page, pairs)),
                pltpu.SemaphoreType.DMA((n_page, pairs)),
                pltpu.SemaphoreType.DMA((n_head, chunks)),
                pltpu.SemaphoreType.DMA((2, n_head, chunks)),
            ],
            compiler_params=pltpu.CompilerParams(
                collective_id=0, has_side_effects=True, vmem_limit_bytes=60 * 1024 * 1024
            ),
            cost_estimate=pl.CostEstimate(
                flops=2 * rows * n_page * inner * columns,
                bytes_accessed=2 * (inner * columns + rows_out * columns),
                transcendentals=0,
            ),
        )(
            block_table,
            ancestor_len,
            queries,
            new_keys,
            new_values,
            cache_keys,
            cache_values,
            out_weight,
        )

    in_specs = (
        P(("branch", "page"), "head"),
        P(("branch", "page"), "head"),
        P(("branch", "page"), "head"),
        P(("branch", "page"), None, "head"),
        P(("branch", "page"), None, "head"),
        P(("branch", "page"), None),
        P(("branch", "page")),
        P("head", "page"),
    )
    out_specs = P(("branch", "head"), "page")
    return jax.shard_map(shards, mesh=mesh, in_specs=in_specs, out_specs=out_specs, check_vma=False)
```

```python
import functools
import math

import jax
import jax.numpy as jnp
from jax import lax
from jax.experimental import pallas as pl
from jax.experimental.pallas import tpu as pltpu
from jax.sharding import PartitionSpec as P

HD = 128
PAGE_TOK = 64
NEW = 256
PAIR = 2
SKEW = 2
MESH = pl.DeviceIdType.MESH


def kernel(
    n_branch,
    n_head,
    n_page,
    width,
    table_ref,
    len_ref,
    q_ref,
    nk_ref,
    nv_ref,
    ck_ref,
    cv_ref,
    w_hbm,
    out_ref,
    k_all,
    v_all,
    k_cat,
    v_cat,
    v_own,
    own_mix,
    own_top,
    attn_all,
    w_ref,
    flow,
    total,
    w_sem,
    kv_send,
    kv_recv,
    attn_send,
    attn_recv,
    flow_send,
    flow_recv,
):
    my_branch = lax.axis_index("branch")
    z = lax.axis_index("head")
    my_page = lax.axis_index("page")
    group = n_branch * n_page
    me = my_branch * n_page + my_page
    rows = q_ref.shape[0]
    heads = q_ref.shape[1] // HD
    branches, slots = table_ref.shape
    pages_here = ck_ref.shape[0]
    ancestors = slots * PAGE_TOK
    rows_out, columns = out_ref.shape
    chunks = columns // width
    pairs = heads // PAIR

    w_copy = pltpu.make_async_copy(w_hbm, w_ref, w_sem)
    w_copy.start()

    def peer_of(k):
        other = lax.rem(me + k, group)
        return other // n_page, lax.rem(other, n_page)

    barrier = pltpu.get_barrier_semaphore()

    @pl.loop(1, group)
    def _(k):
        b, p = peer_of(k)
        pl.semaphore_signal(
            barrier, inc=1, device_id={"branch": b, "page": p}, device_id_type=MESH
        )

    @pl.when(z > 0)
    def _():
        pl.semaphore_signal(barrier, inc=1, device_id={"head": z - 1}, device_id_type=MESH)

    @pl.when(z < n_head - 1)
    def _():
        pl.semaphore_signal(barrier, inc=1, device_id={"head": z + 1}, device_id_type=MESH)

    inner_head = jnp.logical_and(z > 0, z < n_head - 1)
    pl.semaphore_wait(barrier, group - 1 + jnp.where(inner_head, 2, 1))

    def cache_copy(which, k):
        b, p = peer_of(k)
        src, dst = ((ck_ref, k_all), (cv_ref, v_all))[which]
        return pltpu.make_async_remote_copy(
            src_ref=src,
            dst_ref=dst.at[pl.ds(me * pages_here, pages_here)],
            send_sem=kv_send.at[which, k],
            recv_sem=kv_recv.at[which, k],
            device_id={"branch": b, "page": p},
            device_id_type=MESH,
        )

    @pl.loop(1, group)
    def _(k):
        cache_copy(0, k).start()
        cache_copy(1, k).start()

    k_all[pl.ds(me * pages_here, pages_here)] = ck_ref[...]
    v_all[pl.ds(me * pages_here, pages_here)] = cv_ref[...]
    v_cat[:, HD:] = jnp.ones((ancestors, HD), jnp.bfloat16)

    scale = math.log2(math.e) / math.sqrt(HD)

    def softmax_part(scores, floor):
        top = jnp.max(scores, axis=-1, keepdims=True)
        if floor is not None:
            top = jnp.maximum(top, floor)
        return top, jnp.exp2(scores - top).astype(jnp.bfloat16)

    def scores_of(b, lanes, keys):
        return scale * lax.dot_general(
            q_ref[b * NEW : (b + 1) * NEW, lanes],
            keys,
            (((1,), (1,)), ((), ())),
            preferred_element_type=jnp.float32,
        )

    own_row = lax.broadcasted_iota(jnp.int32, (NEW, NEW), 0)
    own_column = lax.broadcasted_iota(jnp.int32, (NEW, NEW), 1)
    own_bias = jnp.where(own_column <= own_row, 0.0, -1e30).astype(jnp.float32)

    for b in range(branches):
        v_own[b, :, :HD] = nv_ref[b * NEW : (b + 1) * NEW]
        v_own[b, :, HD:] = jnp.ones((NEW, HD), jnp.bfloat16)

        @pl.loop(0, pairs)
        def _(j):
            for h in range(PAIR):
                head = j * PAIR + h
                lanes = pl.ds(pl.multiple_of(head * HD, HD), HD)
                top, numer = softmax_part(
                    scores_of(b, lanes, nk_ref[b * NEW : (b + 1) * NEW]) + own_bias, None
                )
                own_mix[b, head] = jnp.dot(numer, v_own[b], preferred_element_type=jnp.float32)
                own_top[b, head] = jnp.broadcast_to(top, (NEW, HD))

    def attn_copy(j, k):
        p = lax.rem(my_page + k, n_page)
        piece = attn_all.at[
            pl.ds(pl.multiple_of(my_page * rows, rows), rows),
            pl.ds(pl.multiple_of(j * PAIR * HD, PAIR * HD), PAIR * HD),
        ]
        return pltpu.make_async_remote_copy(
            src_ref=piece,
            dst_ref=piece,
            send_sem=attn_send.at[k, j],
            recv_sem=attn_recv.at[k, j],
            device_id={"page": p},
            device_id_type=MESH,
        )

    @pl.loop(1, group)
    def _(k):
        cache_copy(0, k).wait_recv()
        cache_copy(1, k).wait_recv()

    column = lax.broadcasted_iota(jnp.int32, (NEW, ancestors), 1)

    for b in range(branches):
        for s in range(slots):
            page_id = table_ref[b, s]
            k_cat[s * PAGE_TOK : (s + 1) * PAGE_TOK] = k_all[page_id]
            v_cat[s * PAGE_TOK : (s + 1) * PAGE_TOK, :HD] = v_all[page_id]
        bias = jnp.where(column < len_ref[b], 0.0, -1e30).astype(jnp.float32)

        @pl.loop(0, pairs)
        def _(j):
            for h in range(PAIR):
                head = j * PAIR + h
                lanes = pl.ds(pl.multiple_of(head * HD, HD), HD)
                before = own_top[b, head][:, :1]
                top, numer = softmax_part(scores_of(b, lanes, k_cat[...]) + bias, before)
                mixed = jnp.dot(numer, v_cat[...], preferred_element_type=jnp.float32)
                mixed = mixed + own_mix[b, head] * jnp.exp2(before - top)
                place = pl.ds(pl.multiple_of(my_page * rows + b * NEW, NEW), NEW)
                attn_all[place, lanes] = (mixed[:, :HD] / mixed[:, HD:]).astype(jnp.bfloat16)
            if b == branches - 1:

                @pl.loop(1, n_page)
                def _(k):
                    attn_copy(j, k).start()

    w_copy.wait()

    def flow_copy(d, c):
        down = jnp.where(d < z, 1, 0)
        return pltpu.make_async_remote_copy(
            src_ref=flow.at[down, d, c],
            dst_ref=flow.at[down, d, c],
            send_sem=flow_send.at[d, c],
            recv_sem=flow_recv.at[down, d, c],
            device_id={"head": jnp.where(d < z, z - 1, z + 1)},
            device_id_type=MESH,
        )

    def incoming(down, d, c):
        return pltpu.make_async_remote_copy(
            src_ref=flow.at[down, d, c],
            dst_ref=flow.at[down, d, c],
            send_sem=flow_send.at[d, c],
            recv_sem=flow_recv.at[down, d, c],
            device_id={"head": jnp.where(z == 0, z + 1, z - 1)},
            device_id_type=MESH,
        )

    phases = n_head // 2
    pages_phase = n_page // phases
    my_phase = my_page // pages_phase
    ticks = (n_head - 1) * chunks

    def stream(tick, going_down):
        dest = piece = jnp.int32(0)
        for first in range(phases):
            start = 0
            for ph in range(phases):
                half = (first + ph) % phases
                dests = [half * 2, half * 2 + 1] if going_down else [half * 2 + 1, half * 2]
                dests = [d for d in dests if d != (n_head - 1 if going_down else 0)]
                here = jnp.logical_and(my_phase == first, tick >= start)
                local = jnp.maximum(tick - start, 0)
                step = 1 if going_down else -1
                dest = jnp.where(here, dests[0] + step * jnp.minimum(local // chunks, len(dests) - 1), dest)
                piece = jnp.where(here, lax.rem(local, chunks), piece)
                start += len(dests) * chunks
        return dest, piece

    def wait_attention(first, count):
        @pl.loop(0, count)
        def _(i):
            source = lax.rem(first + i, n_page)
            k = lax.rem(my_page - source + n_page, n_page)

            @pl.when(k > 0)
            def _():
                @pl.loop(0, pairs)
                def _(j):
                    piece = attn_all.at[
                        pl.ds(pl.multiple_of(source * rows, rows), rows),
                        pl.ds(pl.multiple_of(j * PAIR * HD, PAIR * HD), PAIR * HD),
                    ]
                    pltpu.make_async_remote_copy(
                        src_ref=piece,
                        dst_ref=piece,
                        send_sem=attn_send.at[k, j],
                        recv_sem=attn_recv.at[k, j],
                        device_id={"page": lax.rem(my_page + 1, n_page)},
                        device_id_type=MESH,
                    ).wait_recv()

    def project(d, c):
        return jnp.dot(
            attn_all[pl.ds(pl.multiple_of(d * rows_out, rows_out), rows_out), :],
            w_ref[:, pl.ds(pl.multiple_of(c * width, width), width)],
            preferred_element_type=jnp.float32,
        )

    def event(step, down):
        depth = n_head - 1 - z if down == 1 else z
        tick = step - SKEW * jnp.maximum(depth - 1, 0)
        d, c = stream(tick, down)
        valid = jnp.logical_and(tick >= 0, tick < ticks)
        active = jnp.logical_and(valid, d < z if down == 1 else d > z)
        received = z < n_head - 1 if down == 1 else z > 0
        mine = jnp.logical_and(valid, d == z)
        if down == 1:
            mine = jnp.logical_and(mine, z == 0)

        @pl.when(mine)
        def _():
            total[c] = project(d, c)

        @pl.when(jnp.logical_and(active, received))
        def _():
            part = project(d, c)
            incoming(down, d, c).wait_recv()
            flow[down, d, c] = (part + flow[down, d, c].astype(jnp.float32)).astype(
                jnp.bfloat16
            )
            flow_copy(d, c).start()

        @pl.when(jnp.logical_and(active, jnp.logical_not(received)))
        def _():
            flow[down, d, c] = project(d, c).astype(jnp.bfloat16)
            flow_copy(d, c).start()

    def run(low, high):
        @pl.loop(low, high)
        def _(step):
            @pl.when(z < n_head // 2)
            def _():
                event(step, 0)

            event(step, 1)

            @pl.when(z >= n_head // 2)
            def _():
                event(step, 0)

    wait_attention(my_phase * pages_phase, pages_phase)
    run(0, chunks)
    wait_attention((my_phase + 1) * pages_phase, n_page - pages_phase)
    run(chunks, ticks + SKEW * (n_head - 2))

    @pl.loop(0, chunks)
    def _(c):
        @pl.when(z > 0)
        def _():
            incoming(0, z, c).wait_recv()
            total[c] = total[c] + flow[0, z, c].astype(jnp.float32)

        @pl.when(z < n_head - 1)
        def _():
            incoming(1, z, c).wait_recv()
            total[c] = total[c] + flow[1, z, c].astype(jnp.float32)

        out_ref[:, pl.ds(pl.multiple_of(c * width, width), width)] = total[c].astype(
            jnp.bfloat16
        )

    @pl.loop(1, group)
    def _(k):
        cache_copy(0, k).wait_send()
        cache_copy(1, k).wait_send()

    @pl.loop(1, n_page)
    def _(k):
        @pl.loop(0, pairs)
        def _(j):
            attn_copy(j, k).wait_send()

    @pl.loop(0, n_head * chunks)
    def _(step):
        d = step // chunks
        c = lax.rem(step, chunks)

        @pl.when(d != z)
        def _():
            flow_copy(d, c).wait_send()


def solution(mesh):
    n_branch, n_head, n_page = (mesh.shape[a] for a in ("branch", "head", "page"))

    def shards(
        queries,
        new_keys,
        new_values,
        cache_keys,
        cache_values,
        block_table,
        ancestor_len,
        out_weight,
    ):
        rows, inner = queries.shape
        columns = out_weight.shape[1]
        rows_out = rows * n_page // n_head
        pages = cache_keys.shape[0] * n_branch * n_page
        ancestors = block_table.shape[1] * PAGE_TOK
        branches = block_table.shape[0]
        heads = inner // HD
        width = math.gcd(columns, 256)
        chunks = columns // width
        pairs = inner // HD // PAIR
        group = n_branch * n_page
        vmem = pl.BlockSpec(memory_space=pltpu.VMEM)
        smem = pl.BlockSpec(memory_space=pltpu.SMEM)
        hbm = pl.BlockSpec(memory_space=pl.ANY)
        return pl.pallas_call(
            functools.partial(kernel, n_branch, n_head, n_page, width),
            out_shape=jax.ShapeDtypeStruct((rows_out, columns), jnp.bfloat16),
            in_specs=[smem, smem, vmem, vmem, vmem, vmem, vmem, hbm],
            out_specs=vmem,
            scratch_shapes=[
                pltpu.VMEM((pages, PAGE_TOK, HD), jnp.bfloat16),
                pltpu.VMEM((pages, PAGE_TOK, HD), jnp.bfloat16),
                pltpu.VMEM((ancestors, HD), jnp.bfloat16),
                pltpu.VMEM((ancestors, 2 * HD), jnp.bfloat16),
                pltpu.VMEM((branches, NEW, 2 * HD), jnp.bfloat16),
                pltpu.VMEM((branches, heads, NEW, 2 * HD), jnp.float32),
                pltpu.VMEM((branches, heads, NEW, HD), jnp.float32),
                pltpu.VMEM((rows * n_page, inner), jnp.bfloat16),
                pltpu.VMEM(out_weight.shape, jnp.bfloat16),
                pltpu.VMEM((2, n_head, chunks, rows_out, width), jnp.bfloat16),
                pltpu.VMEM((chunks, rows_out, width), jnp.float32),
                pltpu.SemaphoreType.DMA,
                pltpu.SemaphoreType.DMA((2, group)),
                pltpu.SemaphoreType.DMA((2, group)),
                pltpu.SemaphoreType.DMA((n_page, pairs)),
                pltpu.SemaphoreType.DMA((n_page, pairs)),
                pltpu.SemaphoreType.DMA((n_head, chunks)),
                pltpu.SemaphoreType.DMA((2, n_head, chunks)),
            ],
            compiler_params=pltpu.CompilerParams(
                collective_id=0, has_side_effects=True, vmem_limit_bytes=60 * 1024 * 1024
            ),
            cost_estimate=pl.CostEstimate(
                flops=2 * rows * n_page * inner * columns,
                bytes_accessed=2 * (inner * columns + rows_out * columns),
                transcendentals=0,
            ),
        )(
            block_table,
            ancestor_len,
            queries,
            new_keys,
            new_values,
            cache_keys,
            cache_values,
            out_weight,
        )

    in_specs = (
        P(("branch", "page"), "head"),
        P(("branch", "page"), "head"),
        P(("branch", "page"), "head"),
        P(("branch", "page"), None, "head"),
        P(("branch", "page"), None, "head"),
        P(("branch", "page"), None),
        P(("branch", "page")),
        P("head", "page"),
    )
    out_specs = P(("branch", "head"), "page")
    return jax.shard_map(shards, mesh=mesh, in_specs=in_specs, out_specs=out_specs, check_vma=False)
```

```python
import functools
import math

import jax
import jax.numpy as jnp
from jax import lax
from jax.experimental import pallas as pl
from jax.experimental.pallas import tpu as pltpu
from jax.sharding import PartitionSpec as P

HD = 128
PAGE_TOK = 64
NEW = 256
PAIR = 2
SKEW = 2
MESH = pl.DeviceIdType.MESH


def kernel(
    n_branch,
    n_head,
    n_page,
    width,
    table_ref,
    len_ref,
    q_ref,
    nk_ref,
    nv_ref,
    ck_ref,
    cv_ref,
    w_hbm,
    out_ref,
    late_ref,
    k_all,
    v_all,
    k_cat,
    v_cat,
    v_own,
    own_mix,
    own_top,
    attn_all,
    w_ref,
    flow,
    total,
    w_sem,
    kv_send,
    kv_recv,
    attn_send,
    attn_recv,
    flow_send,
    flow_recv,
):
    my_branch = lax.axis_index("branch")
    z = lax.axis_index("head")
    my_page = lax.axis_index("page")
    group = n_branch * n_page
    me = my_branch * n_page + my_page
    rows = q_ref.shape[0]
    heads = q_ref.shape[1] // HD
    branches, slots = table_ref.shape
    pages_here = ck_ref.shape[0]
    ancestors = slots * PAGE_TOK
    rows_out, columns = out_ref.shape
    chunks = columns // width
    pairs = heads // PAIR

    w_copy = pltpu.make_async_copy(w_hbm, w_ref, w_sem)
    w_copy.start()

    def peer_of(k):
        other = lax.rem(me + k, group)
        return other // n_page, lax.rem(other, n_page)

    barrier = pltpu.get_barrier_semaphore()

    @pl.loop(1, group)
    def _(k):
        b, p = peer_of(k)
        pl.semaphore_signal(
            barrier, inc=1, device_id={"branch": b, "page": p}, device_id_type=MESH
        )

    @pl.when(z > 0)
    def _():
        pl.semaphore_signal(barrier, inc=1, device_id={"head": z - 1}, device_id_type=MESH)

    @pl.when(z < n_head - 1)
    def _():
        pl.semaphore_signal(barrier, inc=1, device_id={"head": z + 1}, device_id_type=MESH)

    inner_head = jnp.logical_and(z > 0, z < n_head - 1)
    pl.semaphore_wait(barrier, group - 1 + jnp.where(inner_head, 2, 1))

    def cache_copy(which, k):
        b, p = peer_of(k)
        src, dst = ((ck_ref, k_all), (cv_ref, v_all))[which]
        return pltpu.make_async_remote_copy(
            src_ref=src,
            dst_ref=dst.at[pl.ds(me * pages_here, pages_here)],
            send_sem=kv_send.at[which, k],
            recv_sem=kv_recv.at[which, k],
            device_id={"branch": b, "page": p},
            device_id_type=MESH,
        )

    @pl.loop(1, group)
    def _(k):
        cache_copy(0, k).start()
        cache_copy(1, k).start()

    k_all[pl.ds(me * pages_here, pages_here)] = ck_ref[...]
    v_all[pl.ds(me * pages_here, pages_here)] = cv_ref[...]
    v_cat[:, HD:] = jnp.ones((ancestors, HD), jnp.bfloat16)

    scale = math.log2(math.e) / math.sqrt(HD)

    def softmax_part(scores, floor):
        top = jnp.max(scores, axis=-1, keepdims=True)
        if floor is not None:
            top = jnp.maximum(top, floor)
        return top, jnp.exp2(scores - top).astype(jnp.bfloat16)

    def scores_of(b, lanes, keys):
        return scale * lax.dot_general(
            q_ref[b * NEW : (b + 1) * NEW, lanes],
            keys,
            (((1,), (1,)), ((), ())),
            preferred_element_type=jnp.float32,
        )

    own_row = lax.broadcasted_iota(jnp.int32, (NEW, NEW), 0)
    own_column = lax.broadcasted_iota(jnp.int32, (NEW, NEW), 1)
    own_bias = jnp.where(own_column <= own_row, 0.0, -1e30).astype(jnp.float32)

    for b in range(branches):
        v_own[b, :, :HD] = nv_ref[b * NEW : (b + 1) * NEW]
        v_own[b, :, HD:] = jnp.ones((NEW, HD), jnp.bfloat16)

        @pl.loop(0, pairs)
        def _(j):
            for h in range(PAIR):
                head = j * PAIR + h
                lanes = pl.ds(pl.multiple_of(head * HD, HD), HD)
                top, numer = softmax_part(
                    scores_of(b, lanes, nk_ref[b * NEW : (b + 1) * NEW]) + own_bias, None
                )
                own_mix[b, head] = jnp.dot(numer, v_own[b], preferred_element_type=jnp.float32)
                own_top[b, head] = jnp.broadcast_to(top, (NEW, HD))

    def attn_copy(j, k):
        p = lax.rem(my_page + k, n_page)
        piece = attn_all.at[
            pl.ds(pl.multiple_of(my_page * rows, rows), rows),
            pl.ds(pl.multiple_of(j * PAIR * HD, PAIR * HD), PAIR * HD),
        ]
        return pltpu.make_async_remote_copy(
            src_ref=piece,
            dst_ref=piece,
            send_sem=attn_send.at[k, j],
            recv_sem=attn_recv.at[k, j],
            device_id={"page": p},
            device_id_type=MESH,
        )

    @pl.loop(1, group)
    def _(k):
        cache_copy(0, k).wait_recv()
        cache_copy(1, k).wait_recv()

    column = lax.broadcasted_iota(jnp.int32, (NEW, ancestors), 1)

    for b in range(branches):
        for s in range(slots):
            page_id = table_ref[b, s]
            k_cat[s * PAGE_TOK : (s + 1) * PAGE_TOK] = k_all[page_id]
            v_cat[s * PAGE_TOK : (s + 1) * PAGE_TOK, :HD] = v_all[page_id]
        bias = jnp.where(column < len_ref[b], 0.0, -1e30).astype(jnp.float32)

        @pl.loop(0, pairs)
        def _(j):
            for h in range(PAIR):
                head = j * PAIR + h
                lanes = pl.ds(pl.multiple_of(head * HD, HD), HD)
                before = own_top[b, head][:, :1]
                top, numer = softmax_part(scores_of(b, lanes, k_cat[...]) + bias, before)
                mixed = jnp.dot(numer, v_cat[...], preferred_element_type=jnp.float32)
                mixed = mixed + own_mix[b, head] * jnp.exp2(before - top)
                place = pl.ds(pl.multiple_of(my_page * rows + b * NEW, NEW), NEW)
                attn_all[place, lanes] = (mixed[:, :HD] / mixed[:, HD:]).astype(jnp.bfloat16)
            if b == branches - 1:

                @pl.loop(1, n_page)
                def _(k):
                    attn_copy(j, k).start()

    w_copy.wait()

    def flow_copy(d, c):
        down = jnp.where(d < z, 1, 0)
        return pltpu.make_async_remote_copy(
            src_ref=flow.at[down, d, c],
            dst_ref=flow.at[down, d, c],
            send_sem=flow_send.at[d, c],
            recv_sem=flow_recv.at[down, d, c],
            device_id={"head": jnp.where(d < z, z - 1, z + 1)},
            device_id_type=MESH,
        )

    def incoming(down, d, c):
        return pltpu.make_async_remote_copy(
            src_ref=flow.at[down, d, c],
            dst_ref=flow.at[down, d, c],
            send_sem=flow_send.at[d, c],
            recv_sem=flow_recv.at[down, d, c],
            device_id={"head": jnp.where(z == 0, z + 1, z - 1)},
            device_id_type=MESH,
        )

    phases = n_head // 2
    pages_phase = n_page // phases
    my_phase = my_page // pages_phase
    ticks = (n_head - 1) * chunks

    def stream(tick, going_down):
        dest = piece = jnp.int32(0)
        for first in range(phases):
            start = 0
            for ph in range(phases):
                half = (first + ph) % phases
                dests = [half * 2, half * 2 + 1] if going_down else [half * 2 + 1, half * 2]
                dests = [d for d in dests if d != (n_head - 1 if going_down else 0)]
                here = jnp.logical_and(my_phase == first, tick >= start)
                local = jnp.maximum(tick - start, 0)
                step = 1 if going_down else -1
                dest = jnp.where(here, dests[0] + step * jnp.minimum(local // chunks, len(dests) - 1), dest)
                piece = jnp.where(here, lax.rem(local, chunks), piece)
                start += len(dests) * chunks
        return dest, piece

    def wait_attention(first, count):
        @pl.loop(0, count)
        def _(i):
            source = lax.rem(first + i, n_page)
            k = lax.rem(my_page - source + n_page, n_page)

            @pl.when(k > 0)
            def _():
                @pl.loop(0, pairs)
                def _(j):
                    piece = attn_all.at[
                        pl.ds(pl.multiple_of(source * rows, rows), rows),
                        pl.ds(pl.multiple_of(j * PAIR * HD, PAIR * HD), PAIR * HD),
                    ]
                    pltpu.make_async_remote_copy(
                        src_ref=piece,
                        dst_ref=piece,
                        send_sem=attn_send.at[k, j],
                        recv_sem=attn_recv.at[k, j],
                        device_id={"page": lax.rem(my_page + 1, n_page)},
                        device_id_type=MESH,
                    ).wait_recv()

    def project(d, c):
        return jnp.dot(
            attn_all[pl.ds(pl.multiple_of(d * rows_out, rows_out), rows_out), :],
            w_ref[:, pl.ds(pl.multiple_of(c * width, width), width)],
            preferred_element_type=jnp.float32,
        )

    def event(step, down):
        depth = n_head - 1 - z if down == 1 else z
        tick = step - SKEW * jnp.maximum(depth - 1, 0)
        d, c = stream(tick, down)
        valid = jnp.logical_and(tick >= 0, tick < ticks)
        active = jnp.logical_and(valid, d < z if down == 1 else d > z)
        received = z < n_head - 1 if down == 1 else z > 0
        mine = jnp.logical_and(valid, d == z)
        if down == 1:
            mine = jnp.logical_and(mine, z == 0)

        @pl.when(mine)
        def _():
            total[c] = project(d, c)

        @pl.when(jnp.logical_and(active, received))
        def _():
            part = project(d, c)
            incoming(down, d, c).wait_recv()
            flow[down, d, c] = (part + flow[down, d, c].astype(jnp.float32)).astype(
                jnp.bfloat16
            )
            flow_copy(d, c).start()

        @pl.when(jnp.logical_and(active, jnp.logical_not(received)))
        def _():
            flow[down, d, c] = project(d, c).astype(jnp.bfloat16)
            flow_copy(d, c).start()

    def run(low, high):
        @pl.loop(low, high)
        def _(step):
            @pl.when(z < n_head // 2)
            def _():
                event(step, 0)

            event(step, 1)

            @pl.when(z >= n_head // 2)
            def _():
                event(step, 0)

    wait_attention(my_phase * pages_phase, pages_phase)
    run(0, chunks)
    wait_attention((my_phase + 1) * pages_phase, n_page - pages_phase)
    run(chunks, ticks + SKEW * (n_head - 2))

    @pl.loop(0, chunks)
    def _(c):
        lanes = pl.ds(pl.multiple_of(c * width, width), width)

        @pl.when(z > 0)
        def _():
            incoming(0, z, c).wait_recv()
            total[c] = total[c] + flow[0, z, c].astype(jnp.float32)

        @pl.when(z < n_head - 1)
        def _():
            incoming(1, z, c).wait_recv()
            late_ref[:, lanes] = flow[1, z, c]

        @pl.when(z == n_head - 1)
        def _():
            late_ref[:, lanes] = jnp.zeros((rows_out, width), jnp.bfloat16)

        out_ref[:, lanes] = total[c].astype(jnp.bfloat16)

    @pl.loop(1, group)
    def _(k):
        cache_copy(0, k).wait_send()
        cache_copy(1, k).wait_send()

    @pl.loop(1, n_page)
    def _(k):
        @pl.loop(0, pairs)
        def _(j):
            attn_copy(j, k).wait_send()

    @pl.loop(0, n_head * chunks)
    def _(step):
        d = step // chunks
        c = lax.rem(step, chunks)

        @pl.when(d != z)
        def _():
            flow_copy(d, c).wait_send()


def solution(mesh):
    n_branch, n_head, n_page = (mesh.shape[a] for a in ("branch", "head", "page"))

    def shards(
        queries,
        new_keys,
        new_values,
        cache_keys,
        cache_values,
        block_table,
        ancestor_len,
        out_weight,
    ):
        rows, inner = queries.shape
        columns = out_weight.shape[1]
        rows_out = rows * n_page // n_head
        pages = cache_keys.shape[0] * n_branch * n_page
        ancestors = block_table.shape[1] * PAGE_TOK
        branches = block_table.shape[0]
        heads = inner // HD
        width = math.gcd(columns, 256)
        chunks = columns // width
        pairs = inner // HD // PAIR
        group = n_branch * n_page
        vmem = pl.BlockSpec(memory_space=pltpu.VMEM)
        smem = pl.BlockSpec(memory_space=pltpu.SMEM)
        hbm = pl.BlockSpec(memory_space=pl.ANY)
        early, late = pl.pallas_call(
            functools.partial(kernel, n_branch, n_head, n_page, width),
            out_shape=[jax.ShapeDtypeStruct((rows_out, columns), jnp.bfloat16)] * 2,
            in_specs=[smem, smem, vmem, vmem, vmem, vmem, vmem, hbm],
            out_specs=[vmem, vmem],
            scratch_shapes=[
                pltpu.VMEM((pages, PAGE_TOK, HD), jnp.bfloat16),
                pltpu.VMEM((pages, PAGE_TOK, HD), jnp.bfloat16),
                pltpu.VMEM((ancestors, HD), jnp.bfloat16),
                pltpu.VMEM((ancestors, 2 * HD), jnp.bfloat16),
                pltpu.VMEM((branches, NEW, 2 * HD), jnp.bfloat16),
                pltpu.VMEM((branches, heads, NEW, 2 * HD), jnp.float32),
                pltpu.VMEM((branches, heads, NEW, HD), jnp.float32),
                pltpu.VMEM((rows * n_page, inner), jnp.bfloat16),
                pltpu.VMEM(out_weight.shape, jnp.bfloat16),
                pltpu.VMEM((2, n_head, chunks, rows_out, width), jnp.bfloat16),
                pltpu.VMEM((chunks, rows_out, width), jnp.float32),
                pltpu.SemaphoreType.DMA,
                pltpu.SemaphoreType.DMA((2, group)),
                pltpu.SemaphoreType.DMA((2, group)),
                pltpu.SemaphoreType.DMA((n_page, pairs)),
                pltpu.SemaphoreType.DMA((n_page, pairs)),
                pltpu.SemaphoreType.DMA((n_head, chunks)),
                pltpu.SemaphoreType.DMA((2, n_head, chunks)),
            ],
            compiler_params=pltpu.CompilerParams(
                collective_id=0, has_side_effects=True, vmem_limit_bytes=60 * 1024 * 1024
            ),
            cost_estimate=pl.CostEstimate(
                flops=2 * rows * n_page * inner * columns,
                bytes_accessed=2 * (inner * columns + rows_out * columns),
                transcendentals=0,
            ),
        )(
            block_table,
            ancestor_len,
            queries,
            new_keys,
            new_values,
            cache_keys,
            cache_values,
            out_weight,
        )
        return (early.astype(jnp.float32) + late.astype(jnp.float32)).astype(jnp.bfloat16)

    in_specs = (
        P(("branch", "page"), "head"),
        P(("branch", "page"), "head"),
        P(("branch", "page"), "head"),
        P(("branch", "page"), None, "head"),
        P(("branch", "page"), None, "head"),
        P(("branch", "page"), None),
        P(("branch", "page")),
        P("head", "page"),
    )
    out_specs = P(("branch", "head"), "page")
    return jax.shard_map(shards, mesh=mesh, in_specs=in_specs, out_specs=out_specs, check_vma=False)
```
